256 devices in a mesh: ctx: 32 (over z, x_hi, core), dp: 8 (over y, x_lo).
Axes of the slice: x: 4 (x_hi: 2, x_lo: 2; x = x_hi * 2 + x_lo), y: 4, z: 8, core: 2. Of those that a mesh axis runs over, the one named last changes fastest.
Arguments:
- latent_values: bfloat16 [8, 4096, 576], P('dp', 'ctx'), may hold values from -6 to 6, as said below
- latent_exponents: int32 [8, 32, 9], P('dp', 'ctx'), may hold values from -1 to 1
- query_nope: bfloat16 [8, 4096, 512], P('dp', 'ctx'), may hold values from -6 to 6
- query_rope: bfloat16 [8, 4096, 256], P('dp', 'ctx'), may hold values from -480 to 480
- key_up: bfloat16 [512, 512], replicated, may hold values from -0.5 to 0.5
- value_up: bfloat16 [512, 512], replicated, may hold values from -0.25 to 0.25
- cotangent: bfloat16 [8, 4096, 512], P('dp', 'ctx'), may hold values from -6 to 6
Outputs:
- attended: bfloat16 [8, 4096, 512], P('dp', 'ctx')
- grad_query_nope: bfloat16 [8, 4096, 512], P('dp', 'ctx')
- grad_query_rope: bfloat16 [8, 4096, 256], P('dp', 'ctx')
- grad_latent: float32 [8, 4096, 576], P('dp', 'ctx')
- grad_weights: float32 [512, 1024], P('ctx', 'dp')
The draws below stay inside these ranges and needn't reach their ends.
Inputs may be any that keep to these rules, and one draw needn't show every extreme that they name: `latent_values`: the last 64 columns of every position are the rotary key, which may be closely aligned with the rotary queries of some positions, so that scores can be large; entries lie in the stated range.
All inputs are finite; a program needn't handle non-finite values.
Results may differ from the reference program's by a relative error of at most 0.025.
Values may be sent and summed in bfloat16 or wider, within the bound.
A program may use at most 128 MiB of HBM per device.

```python
import math
import jax
import jax.numpy as jnp
from jax import lax

LATENT = 512
ROPE = 64
NOPE = 128
VDIM = 128
HEADS = 4
QBLOCK = 128
QGROUP = 64
SEQLEN = 4096
SEQS = 8


def rope_base(key):
    return jnp.clip(jax.random.normal(key, (SEQS, SEQLEN, ROPE), jnp.float32), -6.0, 6.0)


def draw_latent_values(key, part):
    shared = rope_base(key)
    key = jax.random.fold_in(key, 11)
    front = jnp.clip(jax.random.normal(key, (SEQS, SEQLEN, LATENT), jnp.float32), -6.0, 6.0)
    return jnp.concatenate([front, shared], axis=-1).astype(jnp.bfloat16)


def draw_query_rope(key, part):
    key = jax.random.fold_in(key, 12)
    drawn = jnp.clip(jax.random.normal(key, (SEQS, SEQLEN, HEADS, ROPE), jnp.float32), -6.0, 6.0)
    return drawn.reshape(SEQS, SEQLEN, HEADS * ROPE).astype(jnp.bfloat16)


def touch_ends(array, key, smallest, high):
    place = [jax.random.randint(jax.random.fold_in(key, axis), (), 0, length) for axis, length in enumerate(array.shape)]
    widest = array.shape.index(max(array.shape))
    beside = place[:widest] + [(place[widest] + 1) % array.shape[widest]] + place[widest + 1:]
    return array.at[tuple(place)].set(smallest).at[tuple(beside)].set(high)


def shard_levels(own_key, shape, split, least, high):
    loudness, own = 1.0, jax.random.fold_in(own_key, 6)
    for axis_at, parts in split:
        steps = jnp.exp(jax.random.uniform(jax.random.fold_in(own, axis_at), (parts,), jnp.float32, least / len(split), high / len(split)))
        loudness = loudness * jnp.repeat(steps, shape[axis_at] // parts).reshape([-1 if axis == axis_at else 1 for axis in range(len(shape))])
    return loudness


def normal_values(stream_key, extent, spread, bound, pieces=(), dtype=jnp.bfloat16):
    level = shard_levels(stream_key, extent, pieces, -0.22, 0.18) if pieces else 1.0
    array = jax.random.normal(stream_key, extent, jnp.float32) * spread * level
    return jnp.minimum(jnp.maximum(array, -bound), bound).astype(dtype)


def setup_inputs(seed: int = 0) -> dict:
    key_list = jax.random.split(jax.random.key(seed), 8)
    latent_values = draw_latent_values(jax.random.fold_in(key_list[7], 71), 0)
    latent_exponents = touch_ends(jax.random.randint(key_list[1], (SEQS, SEQLEN // QBLOCK, (LATENT + ROPE) // QGROUP), -1, 2), jax.random.fold_in(key_list[1], 1), -1, 1).astype(jnp.int32)
    query_nope = normal_values(key_list[2], (SEQS, SEQLEN, HEADS * NOPE), 1.0, 6.0, ((0, 8), (1, 32)))
    query_rope = draw_query_rope(jax.random.fold_in(key_list[7], 71), 0)
    key_up = normal_values(key_list[4], (LATENT, HEADS * NOPE), NOPE ** -0.5, 0.5)
    value_up = normal_values(key_list[5], (LATENT, HEADS * VDIM), LATENT ** -0.5, 0.25)
    cotangent = normal_values(key_list[6], (SEQS, SEQLEN, HEADS * VDIM), 1.0, 6.0, ((0, 8), (1, 32)))
    return {"latent_values": latent_values, "latent_exponents": latent_exponents, "query_nope": query_nope, "query_rope": query_rope, "key_up": key_up, "value_up": value_up, "cotangent": cotangent}


def expand_scales(values, exponents):
    total = values.shape[0]
    width = values.shape[1]
    factors = jnp.exp2(exponents.astype(jnp.float32))
    blocks = factors.shape[0]
    groups = factors.shape[1]
    shaped = values.reshape(blocks, total // blocks, groups, width // groups)
    return (shaped * factors[:, None, :, None]).reshape(total, width)


def one_sequence(latent_values, latent_exponents, query_nope, query_rope, key_up, value_up, cotangent):
    total = latent_values.shape[0]
    width = latent_values.shape[1]
    factor = (NOPE + ROPE) ** -0.5
    latent = expand_scales(latent_values.astype(jnp.float32), latent_exponents).astype(jnp.bfloat16)
    latent_f = latent.astype(jnp.float32)
    nope_f = latent_f[:, :LATENT]
    key_three = key_up.astype(jnp.float32).reshape(LATENT, HEADS, NOPE)
    value_three = value_up.astype(jnp.float32).reshape(LATENT, HEADS, VDIM)
    query_three = query_nope.astype(jnp.float32).reshape(total, HEADS, NOPE)
    qlat = jnp.einsum('the,dhe->thd', query_three, key_three).astype(jnp.bfloat16)
    qall = jnp.concatenate([qlat, query_rope.reshape(total, HEADS, ROPE)], axis=-1)
    cot_three = cotangent.astype(jnp.float32).reshape(total, HEADS, VDIM)
    qrows = math.gcd(total, 512)
    key_pos = jnp.arange(total)

    def block(carry, index):
        start = index * qrows
        qa = lax.dynamic_slice_in_dim(qall, start, qrows, 0).astype(jnp.float32)
        gb = lax.dynamic_slice_in_dim(cot_three, start, qrows, 0)
        pos = start + jnp.arange(qrows)
        scores = jnp.einsum('thd,kd->htk', qa, latent_f) * factor
        allowed = key_pos[None, None, :] <= pos[None, :, None]
        scores = jnp.where(allowed, scores, -jnp.inf)
        top = jnp.max(scores, axis=-1, keepdims=True)
        lse = top + jnp.log(jnp.sum(jnp.exp(scores - top), axis=-1, keepdims=True))
        prob = jnp.exp(scores - lse)
        weights = prob.astype(jnp.bfloat16).astype(jnp.float32)
        olat = jnp.einsum('htk,kd->thd', weights, nope_f).astype(jnp.bfloat16)
        olat_f = olat.astype(jnp.float32)
        attended = jnp.einsum('thd,dhe->the', olat_f, value_three).astype(jnp.bfloat16)
        dolat = jnp.einsum('the,dhe->thd', gb, value_three).astype(jnp.bfloat16)
        dolat_f = dolat.astype(jnp.float32)
        delta = jnp.sum(dolat_f * olat_f, axis=-1)
        dprob = jnp.einsum('thd,kd->htk', dolat_f, nope_f)
        dscore = (prob * (dprob - delta.T[:, :, None]) * factor).astype(jnp.bfloat16).astype(jnp.float32)
        dqall = jnp.einsum('htk,kd->thd', dscore, latent_f)
        term = jnp.einsum('htk,thd->kd', dscore, qa)
        term_nope = jnp.einsum('htk,thd->kd', weights, dolat_f)
        term = term + jnp.concatenate([term_nope, jnp.zeros((total, ROPE), jnp.float32)], axis=1)
        return carry + term, (attended, olat, dqall[..., :LATENT].astype(jnp.bfloat16), dqall[..., LATENT:].astype(jnp.bfloat16))

    dlat, outs = lax.scan(block, jnp.zeros((total, width), jnp.float32), jnp.arange(total // qrows))
    attended = outs[0].reshape(total, HEADS * VDIM)
    olat = outs[1].reshape(total, HEADS, LATENT).astype(jnp.float32)
    dqlat = outs[2].reshape(total, HEADS, LATENT).astype(jnp.float32)
    grad_rope = outs[3].reshape(total, HEADS * ROPE)
    grad_nope = jnp.einsum('thd,dhe->the', dqlat, key_three).astype(jnp.bfloat16).reshape(total, HEADS * NOPE)
    grad_latent = expand_scales(dlat, latent_exponents)
    grad_key = jnp.einsum('thd,the->dhe', dqlat, query_three).reshape(LATENT, HEADS * NOPE)
    grad_value = jnp.einsum('thd,the->dhe', olat, cot_three).reshape(LATENT, HEADS * VDIM)
    partial_sum = jnp.concatenate([grad_key, grad_value], axis=1)
    return attended, grad_nope, grad_rope, grad_latent, partial_sum


def reference(latent_values, latent_exponents, query_nope, query_rope, key_up, value_up, cotangent):
    def each(items):
        return one_sequence(items[0], items[1], items[2], items[3], key_up, value_up, items[4])

    outs = lax.map(each, (latent_values, latent_exponents, query_nope, query_rope, cotangent))
    return outs[0], outs[1], outs[2], outs[3], jnp.sum(outs[4], axis=0)
```

```python
import math

import jax
import jax.numpy as jnp
from jax import lax
from jax.experimental import pallas as pl
from jax.experimental.pallas import tpu as pltpu
from jax.sharding import PartitionSpec as P

LATENT = 512
ROPE = 64
WIDTH = LATENT + ROPE
HEADS = 4
HEAD = 128
ROWS = 128
HALF = ROWS * HEADS
QROWS = 2 * HALF
Z = 8
KEYS = 2 * ROWS
FACTOR = (HEAD + ROPE) ** -0.5
LOG2E = math.log2(math.e)
NEG = -1e30
PARTS = 2
PROWS = ROWS // PARTS
BF16 = jnp.bfloat16
F32 = jnp.float32


def dot(a, b):
    return jnp.dot(a, b, preferred_element_type=F32)


def transposed(a):
    return a.astype(F32).T.astype(BF16)


def remote(src, dst, send, recv, device):
    return pltpu.make_async_remote_copy(
        src_ref=src,
        dst_ref=dst,
        send_sem=send,
        recv_sem=recv,
        device_id=device,
        device_id_type=pl.DeviceIdType.MESH,
    )


def kernel(
    lat_ref, exp_ref, qn_ref, qr_ref, ku_ref, vu_ref, ct_ref,
    att_ref, gn_ref, gr_ref, gl_ref, gw_ref,
    kv, kt, pqn, pqr, pct, q, qt, do, dot_t, kut, vut,
    s_ref, dp_ref, w_ref, ds_ref, acc, dq, ot, st, pst, fin,
    aown, asend, arecv, gown, gsend, grecv,
    dl, pr, sdn, sup, rdn, rup,
    wg, wa, wb, rb, wc, rc, wd, rd,
    up_s, up_r, dn_s, dn_r, sib_s, sib_r, pq_s, pq_r, mid_s, mid_r,
    ls_s, ls_r, rdn_s, rdn_r, rup_s, rup_r,
    a_s, a_r, b_s, b_r, c_s, c_r, d_s, d_r,
):
    k = lax.axis_index("ctx")
    p = lax.axis_index("dp")
    z, xh, c = k // 4, lax.rem(k // 2, 2), lax.rem(k, 2)
    y, xl = p // 2, lax.rem(p, 2)
    x = xh * 2 + xl

    def at(z_, x_, c_, y_):
        return (z_ * 4 + (x_ // 2) * 2 + c_, y_ * 2 + lax.rem(x_, 2))

    sibling = at(z, x, 1 - c, y)
    partner = at(z, lax.rem(x + 2, 4), c, y)
    above = at(lax.rem(z + 1, Z), x, c, y)
    below = at(lax.rem(z + Z - 1, Z), x, c, y)
    xpeers = [lax.rem(x + d, 4) for d in (1, 2, 3)]
    ypeers = [lax.rem(y + d, 4) for d in (1, 2, 3)]
    zpeers = [lax.rem(z + d, Z) for d in range(1, Z)]

    barrier = pltpu.get_barrier_semaphore()
    peers = [sibling]
    peers += [at(z, v, c, y) for v in xpeers]
    peers += [at(z, x, c, v) for v in ypeers]
    peers += [at(v, x, c, y) for v in zpeers]
    for peer in peers:
        pl.semaphore_signal(barrier, inc=1, device_id=peer, device_id_type=pl.DeviceIdType.MESH)

    st[...] = jnp.zeros_like(st)

    group = lax.broadcasted_iota(jnp.int32, (1, WIDTH), 1) // 64
    exps = jnp.zeros((1, WIDTH), jnp.int32)
    for g in range(WIDTH // 64):
        exps = jnp.where(group == g, exp_ref[0, 0, g], exps)
    scale = jnp.where(exps > 0, 2.0, jnp.where(exps < 0, 0.5, 1.0)).astype(F32)
    kv[z, c] = (lat_ref[0].astype(F32) * scale).astype(BF16)

    pl.semaphore_wait(barrier, len(peers))

    def piece(h):
        return pl.ds(h * PROWS, PROWS)

    def up_copy(block, s, h):
        ref = kv.at[block, c, piece(h)]
        return remote(ref, ref, up_s.at[s - 1, h], up_r.at[s - 1, h], above)

    def dn_copy(block, s, h):
        ref = kv.at[block, c, piece(h)]
        return remote(ref, ref, dn_s.at[s - 1, h], dn_r.at[s - 1, h], below)

    def sib_copy(block, i):
        ref = kv.at[block, c]
        return remote(ref, ref, sib_s.at[i], sib_r.at[i], sibling)

    def up_sent(s):
        return (z <= Z - 2) & (z >= s - 1), jnp.maximum(z - (s - 1), 0)

    def dn_sent(s):
        block = lax.rem(z + s - 1, Z)
        return block <= 2, block

    def up_got(s):
        return z >= s, jnp.maximum(z - s, 0)

    def dn_got(s):
        block = lax.rem(z + s, Z)
        return block <= 2, block

    def dn_used(s):
        return z >= Z - s, jnp.maximum(z + s - Z, 0)

    def send_up(s, h):
        ok, block = up_sent(s)

        @pl.when(ok)
        def _():
            up_copy(block, s, h).start()

    def send_dn(s, h):
        ok, block = dn_sent(s)

        @pl.when(ok)
        def _():
            dn_copy(block, s, h).start()

    for h in range(PARTS):
        send_up(1, h)
        send_dn(1, h)
    sib_copy(z, 0).start()
    query_copies = [
        remote(src.at[0], dst, pq_s.at[i], pq_r.at[i], partner)
        for i, (src, dst) in enumerate(((qn_ref, pqn), (qr_ref, pqr), (ct_ref, pct)))
    ]
    for copy in query_copies:
        copy.start()

    for h in range(HEADS):
        cols = pl.ds(h * HEAD, HEAD)
        kut[cols, :] = transposed(ku_ref[:, cols])
        vut[cols, :] = transposed(vu_ref[:, cols])

    def tables(half, qn, qr, ct):
        rope_t = qr.astype(F32).T
        for h in range(HEADS):
            cols = pl.ds(h * HEAD, HEAD)
            rows = pl.ds(half * HALF + h * HEAD, HEAD)
            qh = qn[:, h * HEAD:(h + 1) * HEAD]
            ch = ct[:, h * HEAD:(h + 1) * HEAD]
            rope_h = rope_t[h * ROPE:(h + 1) * ROPE, :]
            q[rows, pl.ds(0, LATENT)] = dot(qh, kut[cols, :]).astype(BF16)
            q[rows, pl.ds(LATENT, ROPE)] = rope_h.T.astype(BF16)
            qt[pl.ds(0, LATENT), rows] = dot(ku_ref[:, cols], transposed(qh)).astype(BF16)
            qt[pl.ds(LATENT, ROPE), rows] = rope_h.astype(BF16)
            do[rows, :] = dot(ch, vut[cols, :]).astype(BF16)
            dot_t[:, rows] = dot(vu_ref[:, cols], transposed(ch)).astype(BF16)

    tables(0, qn_ref[0], qr_ref[0], ct_ref[0])

    def turn(block):
        kt[block] = transposed(kv[block].reshape(KEYS, WIDTH))

    def forward(block, start, count, first):
        rows = pl.ds(start, count)
        keys = kv[block].reshape(KEYS, WIDTH)
        score = dot(keys, qt[:, rows]) * (FACTOR * LOG2E)
        if first:
            kpos = lax.broadcasted_iota(jnp.int32, (KEYS, count), 0) + xh * KEYS
            lane = lax.rem(lax.broadcasted_iota(jnp.int32, (KEYS, count), 1), ROWS)
            qx = xh if start == 0 else 1 - xh
            score = jnp.where(kpos <= lane + (qx * KEYS + c * ROWS), score, NEG)
        dprob = dot(keys[:, :LATENT], dot_t[:, rows])
        s_ref[block, :, rows] = score
        dp_ref[block, :, rows] = dprob
        top = jnp.max(score, axis=0, keepdims=True)
        if not first:
            old = st[0:1, rows]
            top = jnp.maximum(old, top)
            decay = jnp.exp2(old - top)
        e = jnp.exp2(score - top)
        total = jnp.sum(e, axis=0, keepdims=True)
        delta = jnp.sum(e * dprob, axis=0, keepdims=True)
        mixed = dot(kt[block, pl.ds(0, LATENT)], e.astype(BF16))
        if not first:
            total += st[1:2, rows] * decay
            delta += st[2:3, rows] * decay
            mixed += acc[:, rows] * decay
        st[0:1, rows] = top
        st[1:2, rows] = total
        st[2:3, rows] = delta
        acc[:, rows] = mixed

    def blocks_of(s):
        used, low = dn_used(s)
        count = (z >= s).astype(jnp.int32)
        if s <= 3:
            count += used.astype(jnp.int32)
        high = jnp.maximum(z - s, 0)
        return count, lambda i: jnp.where(i == 0, high, low)

    def forward_step(s, start, count, new):
        blocks, nth = blocks_of(s)

        def body(i, carry):
            if new:
                turn(nth(i))
            forward(nth(i), start, count, False)
            return carry

        lax.fori_loop(0, blocks, body, 0)

    def relay(s):
        for h in range(PARTS):
            got, block = up_got(s)

            @pl.when(got)
            def _():
                up_copy(block, s, h).wait_recv()

            if s < 4:
                send_up(s + 1, h)
            if s <= 3:
                got_dn, block_dn = dn_got(s)

                @pl.when(got_dn)
                def _():
                    dn_copy(block_dn, s, h).wait_recv()

                if s < 3:
                    send_dn(s + 1, h)
        got, block = up_got(s)

        @pl.when(got)
        def _():
            sib_copy(block, s).start()

        if s <= 3:
            used, low = dn_used(s)

            @pl.when(used)
            def _():
                sib_copy(low, 4 + s).start()

    def meet(s):
        got, block = up_got(s)

        @pl.when(got)
        def _():
            sib_copy(block, s).wait_recv()

        if s <= 3:
            used, low = dn_used(s)

            @pl.when(used)
            def _():
                sib_copy(low, 4 + s).wait_recv()

    sib_copy(z, 0).wait_recv()
    turn(z)
    forward(z, 0, HALF, True)
    relay(1)
    meet(1)
    forward_step(1, 0, HALF, True)
    relay(2)
    for copy in query_copies:
        copy.wait_recv()
    tables(1, pqn[...], pqr[...], pct[...])
    forward(z, HALF, HALF, True)
    forward_step(1, HALF, HALF, False)
    relay(3)
    meet(2)
    forward_step(2, 0, QROWS, True)
    relay(4)
    meet(3)
    forward_step(3, 0, QROWS, True)
    meet(4)
    forward_step(4, 0, QROWS, True)

    stats = remote(st, pst, mid_s.at[0], mid_r.at[0], partner)
    stats.start()
    dq[...] = jnp.zeros_like(dq)
    stats.wait_recv()
    for half in range(2):
        rows, other = pl.ds(half * HALF, HALF), pl.ds((1 - half) * HALF, HALF)
        top1, top2 = st[0:1, rows], pst[0:1, other]
        top = jnp.maximum(top1, top2)
        part1, part2 = jnp.exp2(top1 - top), jnp.exp2(top2 - top)
        total = st[1:2, rows] * part1 + pst[1:2, other] * part2
        fin[0:1, rows] = top + jnp.log(total) * LOG2E
        fin[1:2, rows] = (st[2:3, rows] * part1 + pst[2:3, other] * part2) / total
        ot[:, rows] = (acc[:, rows] * (part1 / total)).astype(BF16)

    def store_terms(column, terms):
        yy, xx = column // 2, column % 2
        terms = terms.astype(BF16)
        for zz in range(Z):
            for xxh in range(2):
                for cc in range(2):
                    first = zz * 64 + xxh * 32 + cc * 16
                    wg[cc, xxh * 2 + xx, yy, zz] = terms[first:first + 16, :]

    for h in range(HEADS):
        cols = pl.ds(h * HEAD, HEAD)
        mine, theirs = pl.ds(h * HEAD, HEAD), pl.ds(HALF + h * HEAD, HEAD)
        asend[cols, :] = dot(vut[cols, :], ot[:, theirs]).astype(BF16)
        aown[cols, :] = dot(vut[cols, :], ot[:, mine])
    att_copy = remote(asend, arecv, mid_s.at[1], mid_r.at[1], partner)
    att_copy.start()
    for h in range(HEADS):
        cols = pl.ds(h * HEAD, HEAD)
        mine, theirs = pl.ds(h * HEAD, HEAD), pl.ds(HALF + h * HEAD, HEAD)
        store_terms(4 + h, dot(ot[:, mine], ct_ref[0, :, cols]) + dot(ot[:, theirs], pct[:, cols]))

    def backward(block, carry):
        prob = jnp.exp2(s_ref[block] - fin[0:1, :])
        w_ref[block] = prob.astype(BF16)
        dscore = (prob * (dp_ref[block] - fin[1:2, :]) * FACTOR).astype(BF16)
        ds_ref[block] = dscore
        dq[...] += dot(kt[block], dscore)
        return carry

    lax.fori_loop(0, z + 1, backward, 0)

    ot[...] = dq[pl.ds(0, LATENT), :].astype(BF16)
    for h in range(HEADS):
        cols = pl.ds(h * HEAD, HEAD)
        rope = pl.ds(LATENT + h * ROPE, ROPE)
        mine, theirs = pl.ds(h * HEAD, HEAD), pl.ds(HALF + h * HEAD, HEAD)
        gsend[cols, :] = dot(kut[cols, :], ot[:, theirs]).astype(BF16)
        gown[cols, :] = dot(kut[cols, :], ot[:, mine])
        gsend[rope, :] = dq[pl.ds(LATENT, ROPE), theirs].astype(BF16)
        gown[rope, :] = dq[pl.ds(LATENT, ROPE), mine]
    grad_copy = remote(gsend, grecv, mid_s.at[2], mid_r.at[2], partner)
    grad_copy.start()
    for h in range(HEADS):
        cols = pl.ds(h * HEAD, HEAD)
        mine, theirs = pl.ds(h * HEAD, HEAD), pl.ds(HALF + h * HEAD, HEAD)
        store_terms(h, dot(ot[:, mine], qn_ref[0, :, cols]) + dot(ot[:, theirs], pqn[:, cols]))
    a_copy = remote(wg.at[1 - c], wa, a_s, a_r, sibling)
    a_copy.start()

    def ls_copy(block):
        return remote(dl.at[block, 1 - c], pr.at[block], ls_s.at[block], ls_r.at[block], sibling)

    def latent_terms(block):
        a = dot(ds_ref[block], q[...])
        b = dot(w_ref[block], do[...])
        dl[block, :, :, pl.ds(0, LATENT)] = (
            (a[:, :LATENT] + b).astype(BF16).reshape(2, ROWS, LATENT)
        )
        dl[block, :, :, pl.ds(LATENT, ROPE)] = (
            a[:, LATENT:].astype(BF16).reshape(2, ROWS, ROPE)
        )
        ls_copy(block).start()

    def terms_step(t):
        high, low = z - 5 + t, z - 4 - t
        count = (high >= 0).astype(jnp.int32)
        if t <= 3:
            count += (low >= 0).astype(jnp.int32)

        def body(i, carry):
            latent_terms(jnp.where(i == 0, jnp.maximum(high, 0), jnp.maximum(low, 0)))
            return carry

        lax.fori_loop(0, count, body, 0)

    def down_copy(t, h):
        return remote(
            sdn.at[t - 1, piece(h)], rdn.at[t - 1, piece(h)],
            rdn_s.at[t - 1, h], rdn_r.at[t - 1, h], below,
        )

    def rise_copy(t, h):
        return remote(
            sup.at[t - 1, piece(h)], rup.at[t - 1, piece(h)],
            rup_s.at[t - 1, h], rup_r.at[t - 1, h], above,
        )

    def chip_sum(block, h):
        return dl[block, c, piece(h)].astype(F32) + pr[block, piece(h)].astype(F32)

    def pass_on(t):
        high, low = z - 5 + t, z - 4 - t
        goes_down = high >= 0
        high, low_block = jnp.maximum(high, 0), jnp.maximum(low, 0)

        @pl.when(goes_down)
        def _():
            ls_copy(high).wait_recv()

        if t <= 3:

            @pl.when(low >= 0)
            def _():
                ls_copy(low_block).wait_recv()

        for h in range(PARTS):

            @pl.when(goes_down)
            def _():
                if t >= 2:

                    @pl.when(z <= Z - 2)
                    def _():
                        down_copy(t - 1, h).wait_recv()
                        sdn[t - 1, piece(h)] = (
                            chip_sum(high, h) + rdn[t - 2, piece(h)].astype(F32)
                        ).astype(BF16)

                    @pl.when(z == Z - 1)
                    def _():
                        sdn[t - 1, piece(h)] = chip_sum(high, h).astype(BF16)

                else:
                    sdn[t - 1, piece(h)] = chip_sum(high, h).astype(BF16)
                down_copy(t, h).start()

            if t <= 3:

                @pl.when(low >= 0)
                def _():
                    if t >= 2:
                        rise_copy(t - 1, h).wait_recv()
                        sup[t - 1, piece(h)] = (
                            chip_sum(low_block, h) + rup[t - 2, piece(h)].astype(F32)
                        ).astype(BF16)
                    else:
                        sup[t - 1, piece(h)] = chip_sum(low_block, h).astype(BF16)
                    rise_copy(t, h).start()

                if t >= 2:

                    @pl.when(z + 4 - t <= 2)
                    def _():
                        rise_copy(t - 1, h).wait_recv()
                        sup[t - 1, piece(h)] = rup[t - 2, piece(h)]
                        rise_copy(t, h).start()

    terms_step(1)
    terms_step(2)
    pass_on(1)

    a_copy.wait_recv()
    for i in range(4):
        wb[i] = (wg[c, i].astype(F32) + wa[i].astype(F32)).astype(BF16)
    b_copies = [
        remote(wb.at[v], rb.at[i], b_s.at[i], b_r.at[i], at(z, v, c, y))
        for i, v in enumerate(xpeers)
    ]
    for copy in b_copies:
        copy.start()

    terms_step(3)
    pass_on(2)

    for copy in b_copies:
        copy.wait_recv()
    wc[...] = (
        wb[x].astype(F32) + rb[0].astype(F32) + rb[1].astype(F32) + rb[2].astype(F32)
    ).astype(BF16)
    c_copies = [
        remote(wc.at[v], rc.at[i], c_s.at[i], c_r.at[i], at(z, x, c, v))
        for i, v in enumerate(ypeers)
    ]
    for copy in c_copies:
        copy.start()

    terms_step(4)
    pass_on(3)

    for copy in c_copies:
        copy.wait_recv()
    wd[...] = (
        wc[y].astype(F32) + rc[0].astype(F32) + rc[1].astype(F32) + rc[2].astype(F32)
    ).astype(BF16)
    d_copies = [
        remote(wd.at[v], rd.at[i], d_s.at[i], d_r.at[i], at(v, x, c, y))
        for i, v in enumerate(zpeers)
    ]
    for copy in d_copies:
        copy.start()

    terms_step(5)
    pass_on(4)

    att_copy.wait_recv()
    grad_copy.wait_recv()
    for h in range(HEADS):
        cols = pl.ds(h * HEAD, HEAD)
        att_ref[0, :, cols] = (aown[cols, :] + arecv[cols, :].astype(F32)).T.astype(BF16)
        gn_ref[0, :, cols] = (gown[cols, :] + grecv[cols, :].astype(F32)).T.astype(BF16)
    for h in range(HEADS // 2):
        rows = pl.ds(LATENT + h * HEAD, HEAD)
        cols = pl.ds(h * HEAD, HEAD)
        gr_ref[0, :, cols] = (gown[rows, :] + grecv[rows, :].astype(F32)).T.astype(BF16)

    for copy in d_copies:
        copy.wait_recv()
    summed = wd[z].astype(F32)
    for i in range(Z - 1):
        summed += rd[i].astype(F32)
    gw_ref[...] = summed

    ls_copy(z).wait_recv()
    for h in range(PARTS):
        gl_ref[0, piece(h), :] = chip_sum(z, h)

        @pl.when(z <= Z - 2)
        def _():
            down_copy(4, h).wait_recv()
            gl_ref[0, piece(h), :] += rdn[3, piece(h)].astype(F32)

        @pl.when(z <= 2)
        def _():
            rise_copy(3, h).wait_recv()
            gl_ref[0, piece(h), :] += rup[2, piece(h)].astype(F32)

    gl_ref[0] = gl_ref[0] * scale

    for s in range(1, 5):
        for h in range(PARTS):
            ok, block = up_sent(s)

            @pl.when(ok)
            def _():
                up_copy(block, s, h).wait_send()

            if s <= 3:
                ok_dn, block_dn = dn_sent(s)

                @pl.when(ok_dn)
                def _():
                    dn_copy(block_dn, s, h).wait_send()

                @pl.when(lax.rem(z + 4 - s, Z) <= 2)
                def _():
                    rise_copy(s, h).wait_send()

            @pl.when(z - 5 + s >= 0)
            def _():
                down_copy(s, h).wait_send()

        got, block = up_got(s)

        @pl.when(got)
        def _():
            sib_copy(block, s).wait_send()

        if s <= 3:
            used, low = dn_used(s)

            @pl.when(used)
            def _():
                sib_copy(low, 4 + s).wait_send()

    sib_copy(z, 0).wait_send()

    def sent(block, carry):
        ls_copy(block).wait_send()
        return carry

    lax.fori_loop(0, z + 1, sent, 0)
    for copy in query_copies + [stats, att_copy, grad_copy, a_copy] + b_copies + c_copies + d_copies:
        copy.wait_send()


def shards(latent_values, latent_exponents, query_nope, query_rope, key_up, value_up, cotangent):
    dma = pltpu.SemaphoreType.DMA
    vmem = pl.BlockSpec(memory_space=pltpu.VMEM)
    scratch = [
        ((Z, 2, ROWS, WIDTH), BF16),
        ((Z, WIDTH, KEYS), BF16),
        ((ROWS, HALF), BF16),
        ((ROWS, HALF // 2), BF16),
        ((ROWS, HALF), BF16),
        ((QROWS, WIDTH), BF16),
        ((WIDTH, QROWS), BF16),
        ((QROWS, LATENT), BF16),
        ((LATENT, QROWS), BF16),
        ((HALF, LATENT), BF16),
        ((HALF, LATENT), BF16),
        ((Z, KEYS, QROWS), F32),
        ((Z, KEYS, QROWS), F32),
        ((Z, KEYS, QROWS), BF16),
        ((Z, KEYS, QROWS), BF16),
        ((LATENT, QROWS), F32),
        ((WIDTH, QROWS), F32),
        ((LATENT, QROWS), BF16),
        ((8, QROWS), F32),
        ((8, QROWS), F32),
        ((8, QROWS), F32),
        ((HALF, ROWS), F32),
        ((HALF, ROWS), BF16),
        ((HALF, ROWS), BF16),
        ((HALF + HALF // 2, ROWS), F32),
        ((HALF + HALF // 2, ROWS), BF16),
        ((HALF + HALF // 2, ROWS), BF16),
        ((Z, 2, ROWS, WIDTH), BF16),
        ((Z, ROWS, WIDTH), BF16),
        ((4, ROWS, WIDTH), BF16),
        ((3, ROWS, WIDTH), BF16),
        ((4, ROWS, WIDTH), BF16),
        ((3, ROWS, WIDTH), BF16),
        ((2, 4, 4, Z, 16, 128), BF16),
        ((4, 4, Z, 16, 128), BF16),
        ((4, 4, Z, 16, 128), BF16),
        ((3, 4, Z, 16, 128), BF16),
        ((4, Z, 16, 128), BF16),
        ((3, Z, 16, 128), BF16),
        ((Z, 16, 128), BF16),
        ((Z - 1, 16, 128), BF16),
    ]
    pairs = [
        (4, PARTS), (3, PARTS), (8,), (3,), (3,),
        (Z,), (4, PARTS), (3, PARTS),
        (), (3,), (3,), (Z - 1,),
    ]
    semaphores = []
    for shape in pairs:
        semaphores += [dma(shape) if shape else dma] * 2
    return pl.pallas_call(
        kernel,
        out_shape=(
            jax.ShapeDtypeStruct((1, ROWS, HALF), BF16),
            jax.ShapeDtypeStruct((1, ROWS, HALF), BF16),
            jax.ShapeDtypeStruct((1, ROWS, HALF // 2), BF16),
            jax.ShapeDtypeStruct((1, ROWS, WIDTH), F32),
            jax.ShapeDtypeStruct((16, 128), F32),
        ),
        in_specs=[vmem, pl.BlockSpec(memory_space=pltpu.SMEM)] + [vmem] * 5,
        out_specs=(vmem,) * 5,
        scratch_shapes=[pltpu.VMEM(*spec) for spec in scratch] + semaphores,
        compiler_params=pltpu.CompilerParams(
            collective_id=0, has_side_effects=True, vmem_limit_bytes=60 << 20
        ),
    )(latent_values, latent_exponents, query_nope, query_rope, key_up, value_up, cotangent)


def solution(mesh):
    block = P("dp", "ctx", None)
    return jax.shard_map(
        shards,
        mesh=mesh,
        in_specs=(block, block, block, block, P(), P(), block),
        out_specs=(block, block, block, block, P("ctx", "dp")),
        check_vma=False,
    )
```

```python
import math

import jax
import jax.numpy as jnp
from jax import lax
from jax.experimental import pallas as pl
from jax.experimental.pallas import tpu as pltpu
from jax.sharding import PartitionSpec as P

LATENT = 512
ROPE = 64
WIDTH = LATENT + ROPE
HEADS = 4
HEAD = 128
ROWS = 128
HALF = ROWS * HEADS
QROWS = 2 * HALF
Z = 8
KEYS = 2 * ROWS
FACTOR = (HEAD + ROPE) ** -0.5
LOG2E = math.log2(math.e)
NEG = -1e30
SLOTS = 8
NEEDS = (0, 1, 7, 2, 6, 3, 5, 4)
UP_SLOT = (0, 1, 3, 5, 7)
DN_SLOT = (0, 2, 4, 6, 7)
GPARTS = 2
GROWS = WIDTH // GPARTS
TROWS = ROWS + ROWS * ROPE // LATENT
RPARTS = 3
RROWS = TROWS // RPARTS
BF16 = jnp.bfloat16
F32 = jnp.float32


def dot(a, b):
    return jnp.dot(a, b, preferred_element_type=F32)


def transposed(a):
    return a.astype(F32).T.astype(BF16)


def remote(src, dst, send, recv, device):
    return pltpu.make_async_remote_copy(
        src_ref=src,
        dst_ref=dst,
        send_sem=send,
        recv_sem=recv,
        device_id=device,
        device_id_type=pl.DeviceIdType.MESH,
    )


def kernel(
    lat_hbm, exp_ref, qn_hbm, qr_hbm, ku_hbm, vu_hbm, ct_hbm,
    att_ref, gn_ref, gr_ref, gl_ref, gw_ref,
    lat, qn_ref, qr_ref, ku_ref, vu_ref, ct_ref,
    kt, kk, pqn, pqr, pct, q, qt, do, dot_t, kut, vut,
    s_ref, dp_ref, w_ref, ds_ref, acc, dq, ot, dqt, st, pst, fin,
    aown, asend, arecv, gown, gsend, grecv,
    dl, pr, sdn, sup, rdn, rup, tot,
    wg, wa, wb, rb, wc, rc, wd, rd,
    in_sem,
    up_s, up_r, dn_s, dn_r, sib_s, sib_r, pq_s, pq_r, mid_s, mid_r,
    ls_s, ls_r, rdn_s, rdn_r, rup_s, rup_r,
    a_s, a_r, b_s, b_r, c_s, c_r, d_s, d_r,
):
    k = lax.axis_index("ctx")
    p = lax.axis_index("dp")
    z, xh, c = k // 4, lax.rem(k // 2, 2), lax.rem(k, 2)
    y, xl = p // 2, lax.rem(p, 2)
    x = xh * 2 + xl

    def at(z_, x_, c_, y_):
        return (z_ * 4 + (x_ // 2) * 2 + c_, y_ * 2 + lax.rem(x_, 2))

    sibling = at(z, x, 1 - c, y)
    partner = at(z, lax.rem(x + 2, 4), c, y)
    above = at(lax.rem(z + 1, Z), x, c, y)
    below = at(lax.rem(z + Z - 1, Z), x, c, y)
    xpeers = [lax.rem(x + d, 4) for d in (1, 2, 3)]
    ypeers = [lax.rem(y + d, 4) for d in (1, 2, 3)]
    zpeers = [lax.rem(z + d, Z) for d in range(1, Z)]

    loads = [
        pltpu.make_async_copy(src, dst, in_sem.at[i])
        for i, (src, dst) in enumerate((
            (lat_hbm, lat), (ku_hbm, ku_ref), (vu_hbm, vu_ref),
            (qn_hbm, qn_ref), (qr_hbm, qr_ref), (ct_hbm, ct_ref),
        ))
    ]
    for load in loads:
        load.start()

    barrier = pltpu.get_barrier_semaphore()
    peers = [sibling]
    peers += [at(z, v, c, y) for v in xpeers]
    peers += [at(z, x, c, v) for v in ypeers]
    peers += [at(v, x, c, y) for v in zpeers]
    for peer in peers:
        pl.semaphore_signal(barrier, inc=1, device_id=peer, device_id_type=pl.DeviceIdType.MESH)

    st[...] = jnp.zeros_like(st)

    group = lax.broadcasted_iota(jnp.int32, (WIDTH, ROWS), 0) // 64
    exps = jnp.zeros((WIDTH, ROWS), jnp.int32)
    for g in range(WIDTH // 64):
        exps = jnp.where(group == g, exp_ref[0, 0, g], exps)
    scale = jnp.where(exps > 0, 2.0, jnp.where(exps < 0, 0.5, 1.0)).astype(F32)
    loads[0].wait()
    kt[0, c] = (lat[0].astype(F32) * scale).astype(BF16)

    pl.semaphore_wait(barrier, len(peers))

    def piece(h):
        return pl.ds(h * GROWS, GROWS)

    def up_copy(s, h):
        return remote(
            kt.at[UP_SLOT[s - 1], c, piece(h)], kt.at[UP_SLOT[s], c, piece(h)],
            up_s.at[s - 1, h], up_r.at[s - 1, h], above,
        )

    def dn_copy(s, h):
        return remote(
            kt.at[DN_SLOT[s - 1], c, piece(h)], kt.at[DN_SLOT[s], c, piece(h)],
            dn_s.at[s - 1, h], dn_r.at[s - 1, h], below,
        )

    def sib_copy(slot):
        ref = kt.at[slot, c]
        return remote(ref, ref, sib_s.at[slot], sib_r.at[slot], sibling)

    def up_sent(s):
        ok = (z <= Z - 2) & (z >= s - 1)
        return ok & (c == 0) if s == 4 else ok

    def up_got(s):
        return (z >= s) & (c == 0) if s == 4 else z >= s

    def dn_sent(s):
        ok = lax.rem(z + s - 1, Z) <= 2 + c
        return ok & (c == 1) if s == 4 else ok

    def dn_got(s):
        ok = lax.rem(z + s, Z) <= 2 + c
        return ok & (c == 1) if s == 4 else ok

    for h in range(GPARTS):

        @pl.when(up_sent(1))
        def _():
            up_copy(1, h).start()

        @pl.when(dn_sent(1))
        def _():
            dn_copy(1, h).start()

    sib_copy(0).start()
    for load in loads[1:]:
        load.wait()
    query_copies = [
        remote(src.at[0], dst, pq_s.at[i], pq_r.at[i], partner)
        for i, (src, dst) in enumerate(((qn_ref, pqn), (qr_ref, pqr), (ct_ref, pct)))
    ]
    for copy in query_copies:
        copy.start()

    for h in range(HEADS):
        cols = pl.ds(h * HEAD, HEAD)
        kut[cols, :] = transposed(ku_ref[:, cols])
        vut[cols, :] = transposed(vu_ref[:, cols])

    def tables(half, qn, qr, ct):
        rope_t = qr.astype(F32).T
        for h in range(HEADS):
            cols = pl.ds(h * HEAD, HEAD)
            rows = pl.ds(half * HALF + h * HEAD, HEAD)
            qh = qn[:, h * HEAD:(h + 1) * HEAD]
            ch = ct[:, h * HEAD:(h + 1) * HEAD]
            rope_h = rope_t[h * ROPE:(h + 1) * ROPE, :]
            q[rows, pl.ds(0, LATENT)] = dot(qh, kut[cols, :]).astype(BF16)
            q[rows, pl.ds(LATENT, ROPE)] = rope_h.T.astype(BF16)
            qt[pl.ds(0, LATENT), rows] = dot(ku_ref[:, cols], transposed(qh)).astype(BF16)
            qt[pl.ds(LATENT, ROPE), rows] = rope_h.astype(BF16)
            do[rows, :] = dot(ch, vut[cols, :]).astype(BF16)
            dot_t[:, rows] = dot(vu_ref[:, cols], transposed(ch)).astype(BF16)

    tables(0, qn_ref[0], qr_ref[0], ct_ref[0])

    def relay(s):
        for h in range(GPARTS):

            @pl.when(up_got(s))
            def _():
                up_copy(s, h).wait_recv()
                if s < 4:

                    @pl.when(up_sent(s + 1))
                    def _():
                        up_copy(s + 1, h).start()

            @pl.when(dn_got(s))
            def _():
                dn_copy(s, h).wait_recv()
                if s < 4:

                    @pl.when(dn_sent(s + 1))
                    def _():
                        dn_copy(s + 1, h).start()

        for slot in sorted({UP_SLOT[s], DN_SLOT[s]}):

            @pl.when(z >= NEEDS[slot])
            def _():
                sib_copy(slot).start()

    def meet(s):
        for slot in sorted({UP_SLOT[s], DN_SLOT[s]}):

            @pl.when(z >= NEEDS[slot])
            def _():
                sib_copy(slot).wait_recv()
                turn(slot)

    def turn(slot):
        for cc in range(2):
            kk[pl.ds(slot * KEYS + cc * ROWS, ROWS), :] = transposed(kt[slot, cc])

    def columns(slot, count, width):
        return jnp.concatenate(
            [kt[slot + i, cc, :width] for i in range(count) for cc in range(2)], axis=1
        )

    def forward(half, slot, count):
        rows = pl.ds(half * HALF, HALF)
        keys = pl.ds(slot * KEYS, count * KEYS)
        score = dot(kk[keys, :], qt[:, rows]) * (FACTOR * LOG2E)
        if slot == 0:
            kpos = lax.broadcasted_iota(jnp.int32, (KEYS, HALF), 0) + xh * KEYS
            lane = lax.rem(lax.broadcasted_iota(jnp.int32, (KEYS, HALF), 1), ROWS)
            qx = 1 - xh if half else xh
            score = jnp.where(kpos <= lane + (qx * KEYS + c * ROWS), score, NEG)
        dprob = dot(kk[keys, pl.ds(0, LATENT)], dot_t[:, rows])
        s_ref[keys, rows] = score
        dp_ref[keys, rows] = dprob
        top = jnp.max(score, axis=0, keepdims=True)
        if slot:
            old = st[0:1, rows]
            top = jnp.maximum(old, top)
            decay = jnp.exp2(old - top)
        e = jnp.exp2(score - top)
        total = jnp.sum(e, axis=0, keepdims=True)
        delta = jnp.sum(e * dprob, axis=0, keepdims=True)
        mixed = dot(columns(slot, count, LATENT), e.astype(BF16))
        if slot:
            total += st[1:2, rows] * decay
            delta += st[2:3, rows] * decay
            mixed += acc[:, rows] * decay
        st[0:1, rows] = top
        st[1:2, rows] = total
        st[2:3, rows] = delta
        acc[:, rows] = mixed

    def over(slot, work):
        @pl.when(z >= NEEDS[slot + 1])
        def _():
            work(slot, 2)

        @pl.when((z >= NEEDS[slot]) & (z < NEEDS[slot + 1]))
        def _():
            work(slot, 1)

    def both(slot, count):
        forward(0, slot, count)
        forward(1, slot, count)

    sib_copy(0).wait_recv()
    turn(0)
    forward(0, 0, 1)
    relay(1)
    meet(1)
    over(1, lambda slot, count: forward(0, slot, count))
    relay(2)
    for copy in query_copies:
        copy.wait_recv()
    tables(1, pqn[...], pqr[...], pct[...])
    forward(1, 0, 1)
    over(1, lambda slot, count: forward(1, slot, count))
    relay(3)
    meet(2)
    over(3, both)
    relay(4)
    meet(3)
    over(5, both)
    meet(4)

    @pl.when(z >= NEEDS[7])
    def _():
        both(7, 1)

    stats = remote(st, pst, mid_s.at[0], mid_r.at[0], partner)
    stats.start()
    dq[...] = jnp.zeros_like(dq)
    stats.wait_recv()
    for half in range(2):
        rows, other = pl.ds(half * HALF, HALF), pl.ds((1 - half) * HALF, HALF)
        top1, top2 = st[0:1, rows], pst[0:1, other]
        top = jnp.maximum(top1, top2)
        part1, part2 = jnp.exp2(top1 - top), jnp.exp2(top2 - top)
        total = st[1:2, rows] * part1 + pst[1:2, other] * part2
        fin[0:1, rows] = top + jnp.log(total) * LOG2E
        fin[1:2, rows] = (st[2:3, rows] * part1 + pst[2:3, other] * part2) / total
        ot[:, rows] = (acc[:, rows] * (part1 / total)).astype(BF16)

    def store_terms(column, terms):
        yy, xx = column // 2, column % 2
        terms = terms.astype(BF16)
        for zz in range(Z):
            for xxh in range(2):
                for cc in range(2):
                    first = zz * 64 + xxh * 32 + cc * 16
                    wg[cc, yy, xxh * 2 + xx, zz] = terms[first:first + 16, :]

    def backward(slot, count):
        keys = pl.ds(slot * KEYS, count * KEYS)
        cols = columns(slot, count, WIDTH)
        for half in range(2):
            rows = pl.ds(half * HALF, HALF)
            prob = jnp.exp2(s_ref[keys, rows] - fin[0:1, rows])
            w_ref[keys, rows] = prob.astype(BF16)
            dscore = (prob * (dp_ref[keys, rows] - fin[1:2, rows]) * FACTOR).astype(BF16)
            ds_ref[keys, rows] = dscore
            dq[:, rows] += dot(cols, dscore)

    def ls_copy(slot):
        return remote(dl.at[slot, 1 - c], pr.at[slot], ls_s.at[slot], ls_r.at[slot], sibling)

    def latent_terms(slot, count):
        keys = pl.ds(slot * KEYS, count * KEYS)
        a = dot(ds_ref[keys, :], q[...])
        b = dot(w_ref[keys, :], do[...])
        front = (a[:, :LATENT] + b).astype(BF16)
        for i in range(count):
            for cc in range(2):
                first = i * KEYS + cc * ROWS
                dl[slot + i, cc, pl.ds(0, ROWS), :] = front[first:first + ROWS, :]
                rope = a[first:first + ROWS, LATENT:]
                for j in range(4):
                    pair = [rope[j * 32 + n * 16:j * 32 + n * 16 + 16, :] for n in range(2)]
                    dl[slot + i, cc, pl.ds(ROWS, 16), pl.ds(j * 128, 128)] = jnp.concatenate(
                        pair, axis=1
                    ).astype(BF16)
        for i in range(count):
            ls_copy(slot + i).start()

    def strip(h):
        return pl.ds(h * RROWS, RROWS)

    def down_copy(t, h):
        return remote(
            sdn.at[t - 1, strip(h)], rdn.at[t - 1, strip(h)],
            rdn_s.at[t - 1, h], rdn_r.at[t - 1, h], below,
        )

    def rise_copy(t, h, src=None):
        return remote(
            sup.at[t - 1, strip(h)] if src is None else src, rup.at[t - 1, strip(h)],
            rup_s.at[t - 1, h], rup_r.at[t - 1, h], above,
        )

    def chip_sum(slot, h):
        return dl[slot, c, strip(h)].astype(F32) + pr[slot, strip(h)].astype(F32)

    def down_sent(t):
        return (z >= 4) & (c == 0) if t == 1 else z >= 5 - t

    def rise_sent(t):
        ok = lax.rem(z + 5 - t, Z) <= 2 + c
        return ok & (c == 1) if t == 1 else ok

    def pass_on(t):
        down_slot, rise_slot = UP_SLOT[5 - t], DN_SLOT[5 - t]
        for slot in sorted({down_slot, rise_slot}):

            @pl.when(z >= NEEDS[slot])
            def _():
                ls_copy(slot).wait_recv()

        for h in range(RPARTS):

            @pl.when(down_sent(t))
            def _():
                if t == 1:
                    sdn[t - 1, strip(h)] = chip_sum(down_slot, h).astype(BF16)
                else:
                    more = (z <= Z - 2) & (c == 0) if t == 2 else z <= Z - 2

                    @pl.when(more)
                    def _():
                        down_copy(t - 1, h).wait_recv()
                        sdn[t - 1, strip(h)] = (
                            chip_sum(down_slot, h) + rdn[t - 2, strip(h)].astype(F32)
                        ).astype(BF16)

                    @pl.when(jnp.logical_not(more))
                    def _():
                        sdn[t - 1, strip(h)] = chip_sum(down_slot, h).astype(BF16)

                down_copy(t, h).start()

            @pl.when(rise_sent(t))
            def _():
                if t == 1:
                    sup[t - 1, strip(h)] = chip_sum(rise_slot, h).astype(BF16)
                    rise_copy(t, h).start()
                else:
                    more = c == 1 if t == 2 else c >= 0
                    adds = z >= t + 3

                    @pl.when(more)
                    def _():
                        rise_copy(t - 1, h).wait_recv()

                    @pl.when(adds & more)
                    def _():
                        sup[t - 1, strip(h)] = (
                            chip_sum(rise_slot, h) + rup[t - 2, strip(h)].astype(F32)
                        ).astype(BF16)
                        rise_copy(t, h).start()

                    @pl.when(adds & jnp.logical_not(more))
                    def _():
                        sup[t - 1, strip(h)] = chip_sum(rise_slot, h).astype(BF16)
                        rise_copy(t, h).start()

                    @pl.when(jnp.logical_not(adds))
                    def _():
                        rise_copy(t, h, rup.at[t - 2, strip(h)]).start()

    def chain(slot, count):
        backward(slot, count)
        latent_terms(slot, count)

    def sides(h):
        return pl.ds(h * HEAD, HEAD), pl.ds(HALF + h * HEAD, HEAD)

    a_copies = [
        remote(wg.at[1 - c, pl.ds(2 * i, 2)], wa.at[pl.ds(2 * i, 2)], a_s.at[i], a_r.at[i], sibling)
        for i in range(2)
    ]

    def b_copy(v):
        return remote(wb.at[v], rb.at[y], b_s.at[v], b_r.at[y], at(z, x, c, v))

    def b_wait(v):
        return remote(wb.at[v], rb.at[v], b_s.at[v], b_r.at[v], at(z, x, c, v))

    def chip_weights(i):
        a_copies[i].wait_recv()
        for v in (2 * i, 2 * i + 1):
            wb[v] = (wg[c, v].astype(F32) + wa[v].astype(F32)).astype(BF16)

            @pl.when(y != v)
            def _():
                b_copy(v).start()

    c_copies = [
        remote(wc.at[v], rc.at[i], c_s.at[i], c_r.at[i], at(z, v, c, y))
        for i, v in enumerate(xpeers)
    ]
    d_copies = [
        remote(wd.at[v], rd.at[i], d_s.at[i], d_r.at[i], at(v, x, c, y))
        for i, v in enumerate(zpeers)
    ]

    def row_weights():
        for v in ypeers:
            b_wait(v).wait_recv()
        wc[...] = (
            wb[y].astype(F32) + rb[ypeers[0]].astype(F32)
            + rb[ypeers[1]].astype(F32) + rb[ypeers[2]].astype(F32)
        ).astype(BF16)
        for copy in c_copies:
            copy.start()

    def column_weights():
        for copy in c_copies:
            copy.wait_recv()
        wd[...] = (
            wc[x].astype(F32) + rc[0].astype(F32) + rc[1].astype(F32) + rc[2].astype(F32)
        ).astype(BF16)
        for copy in d_copies:
            copy.start()

    def value_terms():
        for h in range(HEADS):
            cols = pl.ds(h * HEAD, HEAD)
            mine, theirs = sides(h)
            store_terms(
                4 + h, dot(ot[:, mine], ct_ref[0, :, cols]) + dot(ot[:, theirs], pct[:, cols])
            )
        a_copies[1].start()

    def key_terms():
        dqt[...] = dq[pl.ds(0, LATENT), :].astype(BF16)
        for h in range(HEADS):
            cols = pl.ds(h * HEAD, HEAD)
            mine, theirs = sides(h)
            store_terms(
                h, dot(dqt[:, mine], qn_ref[0, :, cols]) + dot(dqt[:, theirs], pqn[:, cols])
            )
        a_copies[0].start()

    att_copy = remote(asend, arecv, mid_s.at[1], mid_r.at[1], partner)
    grad_copy = remote(gsend, grecv, mid_s.at[2], mid_r.at[2], partner)

    def share_output():
        for h in range(HEADS):
            cols = pl.ds(h * HEAD, HEAD)
            mine, theirs = sides(h)
            asend[cols, :] = dot(vut[cols, :], ot[:, theirs]).astype(BF16)
            aown[cols, :] = dot(vut[cols, :], ot[:, mine])
        att_copy.start()

    def share_grads():
        for h in range(HEADS):
            cols = pl.ds(h * HEAD, HEAD)
            rope = pl.ds(LATENT + h * ROPE, ROPE)
            mine, theirs = sides(h)
            gsend[cols, :] = dot(kut[cols, :], dqt[:, theirs]).astype(BF16)
            gown[cols, :] = dot(kut[cols, :], dqt[:, mine])
            gsend[rope, :] = dq[pl.ds(LATENT, ROPE), theirs].astype(BF16)
            gown[rope, :] = dq[pl.ds(LATENT, ROPE), mine]
        grad_copy.start()

    @pl.when(z >= NEEDS[7])
    def _():
        chain(7, 1)

    over(5, backward)
    over(3, backward)
    pass_on(1)
    over(1, backward)
    backward(0, 1)
    key_terms()
    value_terms()
    over(5, latent_terms)
    chip_weights(0)
    chip_weights(1)
    share_output()
    share_grads()
    pass_on(2)
    over(3, latent_terms)
    over(1, latent_terms)
    latent_terms(0, 1)
    pass_on(3)
    row_weights()
    pass_on(4)
    column_weights()

    att_copy.wait_recv()
    grad_copy.wait_recv()
    for h in range(HEADS):
        cols = pl.ds(h * HEAD, HEAD)
        att_ref[0, :, cols] = (aown[cols, :] + arecv[cols, :].astype(F32)).T.astype(BF16)
        gn_ref[0, :, cols] = (gown[cols, :] + grecv[cols, :].astype(F32)).T.astype(BF16)
    for h in range(HEADS // 2):
        rows = pl.ds(LATENT + h * HEAD, HEAD)
        cols = pl.ds(h * HEAD, HEAD)
        gr_ref[0, :, cols] = (gown[rows, :] + grecv[rows, :].astype(F32)).T.astype(BF16)

    for copy in d_copies:
        copy.wait_recv()
    summed = wd[z].astype(F32)
    for i in range(Z - 1):
        summed += rd[i].astype(F32)
    gw_ref[...] = summed

    ls_copy(0).wait_recv()
    for h in range(RPARTS):
        tot[strip(h), :] = chip_sum(0, h)

        @pl.when(z <= Z - 2)
        def _():
            down_copy(4, h).wait_recv()
            tot[strip(h), :] += rdn[3, strip(h)].astype(F32)

        @pl.when(z <= 2 + c)
        def _():
            rise_copy(4, h).wait_recv()
            tot[strip(h), :] += rup[3, strip(h)].astype(F32)

    folded = tot[pl.ds(ROWS, 16), :]
    rope = jnp.concatenate(
        [folded[:, j * ROPE:(j + 1) * ROPE] for j in range(LATENT // ROPE)], axis=0
    )
    gl_ref[0, pl.ds(0, LATENT), :] = tot[pl.ds(0, ROWS), :].T * scale[:LATENT, :]
    gl_ref[0, pl.ds(LATENT, ROPE), :] = rope.T * scale[LATENT:, :]

    for s in range(1, 5):
        for h in range(GPARTS):

            @pl.when(up_sent(s))
            def _():
                up_copy(s, h).wait_send()

            @pl.when(dn_sent(s))
            def _():
                dn_copy(s, h).wait_send()

        for h in range(RPARTS):

            @pl.when(down_sent(s))
            def _():
                down_copy(s, h).wait_send()

            @pl.when(rise_sent(s))
            def _():
                rise_copy(s, h).wait_send()

    for slot in range(SLOTS):

        @pl.when(z >= NEEDS[slot])
        def _():
            sib_copy(slot).wait_send()
            ls_copy(slot).wait_send()

    for v in range(4):

        @pl.when(y != v)
        def _():
            b_copy(v).wait_send()

    for copy in query_copies + [stats, att_copy, grad_copy] + a_copies + c_copies + d_copies:
        copy.wait_send()


def shards(latent_values, latent_exponents, query_nope, query_rope, key_up, value_up, cotangent):
    dma = pltpu.SemaphoreType.DMA
    vmem = pl.BlockSpec(memory_space=pltpu.VMEM)
    scratch = [
        ((1, WIDTH, ROWS), BF16),
        ((1, ROWS, HALF), BF16),
        ((1, ROWS, HALF // 2), BF16),
        ((LATENT, HALF), BF16),
        ((LATENT, HALF), BF16),
        ((1, ROWS, HALF), BF16),
        ((SLOTS, 2, WIDTH, ROWS), BF16),
        ((SLOTS * KEYS, WIDTH), BF16),
        ((ROWS, HALF), BF16),
        ((ROWS, HALF // 2), BF16),
        ((ROWS, HALF), BF16),
        ((QROWS, WIDTH), BF16),
        ((WIDTH, QROWS), BF16),
        ((QROWS, LATENT), BF16),
        ((LATENT, QROWS), BF16),
        ((HALF, LATENT), BF16),
        ((HALF, LATENT), BF16),
        ((SLOTS * KEYS, QROWS), F32),
        ((SLOTS * KEYS, QROWS), F32),
        ((SLOTS * KEYS, QROWS), BF16),
        ((SLOTS * KEYS, QROWS), BF16),
        ((LATENT, QROWS), F32),
        ((WIDTH, QROWS), F32),
        ((LATENT, QROWS), BF16),
        ((LATENT, QROWS), BF16),
        ((8, QROWS), F32),
        ((8, QROWS), F32),
        ((8, QROWS), F32),
        ((HALF, ROWS), F32),
        ((HALF, ROWS), BF16),
        ((HALF, ROWS), BF16),
        ((HALF + HALF // 2, ROWS), F32),
        ((HALF + HALF // 2, ROWS), BF16),
        ((HALF + HALF // 2, ROWS), BF16),
        ((SLOTS, 2, TROWS, LATENT), BF16),
        ((SLOTS, TROWS, LATENT), BF16),
        ((4, TROWS, LATENT), BF16),
        ((4, TROWS, LATENT), BF16),
        ((4, TROWS, LATENT), BF16),
        ((4, TROWS, LATENT), BF16),
        ((TROWS, LATENT), F32),
        ((2, 4, 4, Z, 16, 128), BF16),
        ((4, 4, Z, 16, 128), BF16),
        ((4, 4, Z, 16, 128), BF16),
        ((4, 4, Z, 16, 128), BF16),
        ((4, Z, 16, 128), BF16),
        ((3, Z, 16, 128), BF16),
        ((Z, 16, 128), BF16),
        ((Z - 1, 16, 128), BF16),
    ]
    pairs = [
        (4, GPARTS), (4, GPARTS), (SLOTS,), (3,), (3,),
        (SLOTS,), (4, RPARTS), (4, RPARTS),
        (2,), (4,), (3,), (Z - 1,),
    ]
    semaphores = [dma((6,))]
    for shape in pairs:
        semaphores += [dma(shape)] * 2
    hbm = pl.BlockSpec(memory_space=pl.ANY)
    outs = pl.pallas_call(
        kernel,
        out_shape=(
            jax.ShapeDtypeStruct((1, ROWS, HALF), BF16),
            jax.ShapeDtypeStruct((1, ROWS, HALF), BF16),
            jax.ShapeDtypeStruct((1, ROWS, HALF // 2), BF16),
            jax.ShapeDtypeStruct((1, WIDTH, ROWS), F32),
            jax.ShapeDtypeStruct((16, 128), F32),
        ),
        in_specs=[hbm, pl.BlockSpec(memory_space=pltpu.SMEM)] + [hbm] * 5,
        out_specs=(vmem,) * 5,
        scratch_shapes=[pltpu.VMEM(*spec) for spec in scratch] + semaphores,
        compiler_params=pltpu.CompilerParams(
            collective_id=0, has_side_effects=True, vmem_limit_bytes=60 << 20
        ),
    )(
        jnp.swapaxes(latent_values, 1, 2), latent_exponents,
        query_nope, query_rope, key_up, value_up, cotangent,
    )
    return outs[:3] + (jnp.swapaxes(outs[3], 1, 2), outs[4])


def solution(mesh):
    block = P("dp", "ctx", None)
    return jax.shard_map(
        shards,
        mesh=mesh,
        in_specs=(block, block, block, block, P(), P(), block),
        out_specs=(block, block, block, block, P("ctx", "dp")),
        check_vma=False,
    )
```

```python
import math

import jax
import jax.numpy as jnp
from jax import lax
from jax.experimental import pallas as pl
from jax.experimental.pallas import tpu as pltpu
from jax.sharding import PartitionSpec as P

LATENT = 512
ROPE = 64
WIDTH = LATENT + ROPE
HEADS = 4
HEAD = 128
ROWS = 128
HALF = ROWS * HEADS
QROWS = 2 * HALF
Z = 8
KEYS = 2 * ROWS
FACTOR = (HEAD + ROPE) ** -0.5
LOG2E = math.log2(math.e)
NEG = -1e30
SLOTS = 8
NEEDS = (0, 1, 7, 2, 6, 3, 5, 4)
UP_SLOT = (0, 1, 3, 5, 7)
DN_SLOT = (0, 2, 4, 6, 7)
GPARTS = 3
GROWS = WIDTH // GPARTS
TROWS = ROWS + ROWS * ROPE // LATENT
RPARTS = 3
RROWS = TROWS // RPARTS
BF16 = jnp.bfloat16
F32 = jnp.float32


def dot(a, b):
    return jnp.dot(a, b, preferred_element_type=F32)


def transposed(a):
    return a.astype(F32).T.astype(BF16)


def remote(src, dst, send, recv, device):
    return pltpu.make_async_remote_copy(
        src_ref=src,
        dst_ref=dst,
        send_sem=send,
        recv_sem=recv,
        device_id=device,
        device_id_type=pl.DeviceIdType.MESH,
    )


def kernel(
    lat_hbm, exp_ref, qn_hbm, qr_hbm, ku_hbm, vu_hbm, ct_hbm,
    att_ref, gn_ref, gr_ref, gl_ref, gw_ref,
    lat, qn_ref, qr_ref, ku_ref, vu_ref, ct_ref,
    kt, kk, pqn, pqr, pct, q, qt, do, dot_t, kut, vut,
    s_ref, dp_ref, w_ref, ds_ref, acc, dq, ot, dqt, st, pst, fin,
    aown, asend, arecv, gown, gsend, grecv,
    dl, pr, sdn, sup, rdn, rup, tot,
    wg, wa, wb, rb, wc, rc, wd, rd,
    in_sem,
    up_s, up_r, dn_s, dn_r, sib_s, sib_r, pq_s, pq_r, mid_s, mid_r,
    ls_s, ls_r, rdn_s, rdn_r, rup_s, rup_r,
    a_s, a_r, b_s, b_r, c_s, c_r, d_s, d_r,
):
    k = lax.axis_index("ctx")
    p = lax.axis_index("dp")
    z, xh, c = k // 4, lax.rem(k // 2, 2), lax.rem(k, 2)
    y, xl = p // 2, lax.rem(p, 2)
    x = xh * 2 + xl

    def at(z_, x_, c_, y_):
        return (z_ * 4 + (x_ // 2) * 2 + c_, y_ * 2 + lax.rem(x_, 2))

    sibling = at(z, x, 1 - c, y)
    partner = at(z, lax.rem(x + 2, 4), c, y)
    above = at(lax.rem(z + 1, Z), x, c, y)
    below = at(lax.rem(z + Z - 1, Z), x, c, y)
    xpeers = [lax.rem(x + d, 4) for d in (1, 2, 3)]
    ypeers = [lax.rem(y + d, 4) for d in (1, 2, 3)]
    zpeers = [lax.rem(z + d, Z) for d in range(1, Z)]

    loads = [
        pltpu.make_async_copy(src, dst, in_sem.at[i])
        for i, (src, dst) in enumerate((
            (lat_hbm, lat), (ku_hbm, ku_ref), (vu_hbm, vu_ref),
            (qn_hbm, qn_ref), (qr_hbm, qr_ref), (ct_hbm, ct_ref),
        ))
    ]
    loads[0].start()

    barrier = pltpu.get_barrier_semaphore()
    peers = [at(lax.rem(z + d, Z), x, c, y) for d in (4, 3, 5, 2, 6, 1, 7)]
    peers += [at(z, v, c, y) for v in xpeers]
    peers += [at(z, x, c, v) for v in ypeers]
    peers += [sibling]
    for peer in peers:
        pl.semaphore_signal(barrier, inc=1, device_id=peer, device_id_type=pl.DeviceIdType.MESH)

    for load in loads[1:]:
        load.start()

    st[...] = jnp.zeros_like(st)

    group = lax.broadcasted_iota(jnp.int32, (WIDTH, ROWS), 0) // 64
    exps = jnp.zeros((WIDTH, ROWS), jnp.int32)
    for g in range(WIDTH // 64):
        exps = jnp.where(group == g, exp_ref[0, 0, g], exps)
    scale = jnp.where(exps > 0, 2.0, jnp.where(exps < 0, 0.5, 1.0)).astype(F32)
    loads[0].wait()
    kt[0, c] = (lat[0].astype(F32) * scale).astype(BF16)

    pl.semaphore_wait(barrier, len(peers))

    def piece(h):
        return pl.ds(h * GROWS, GROWS)

    def up_copy(s, h):
        return remote(
            kt.at[UP_SLOT[s - 1], c, piece(h)], kt.at[UP_SLOT[s], c, piece(h)],
            up_s.at[s - 1], up_r.at[s - 1, h], above,
        )

    def dn_copy(s, h):
        return remote(
            kt.at[DN_SLOT[s - 1], c, piece(h)], kt.at[DN_SLOT[s], c, piece(h)],
            dn_s.at[s - 1], dn_r.at[s - 1, h], below,
        )

    def sib_copy(slot):
        ref = kt.at[slot, c]
        return remote(ref, ref, sib_s.at[slot], sib_r.at[slot], sibling)

    def up_sent(s):
        ok = (z <= Z - 2) & (z >= s - 1)
        return ok & (c == 0) if s == 4 else ok

    def up_got(s):
        return (z >= s) & (c == 0) if s == 4 else z >= s

    def dn_sent(s):
        ok = lax.rem(z + s - 1, Z) <= 2 + c
        return ok & (c == 1) if s == 4 else ok

    def dn_got(s):
        ok = lax.rem(z + s, Z) <= 2 + c
        return ok & (c == 1) if s == 4 else ok

    for h in range(GPARTS):

        @pl.when(up_sent(1))
        def _():
            up_copy(1, h).start()

        @pl.when(dn_sent(1))
        def _():
            dn_copy(1, h).start()

    sib_copy(0).start()
    for load in loads[1:]:
        load.wait()
    query_copies = [
        remote(src.at[0], dst, pq_s.at[i], pq_r.at[i], partner)
        for i, (src, dst) in enumerate(((qn_ref, pqn), (qr_ref, pqr), (ct_ref, pct)))
    ]
    for copy in query_copies:
        copy.start()

    def tables(half, qn, qr, ct):
        rope_t = qr.astype(F32).T.astype(BF16)
        for h in range(HEADS):
            cols = pl.ds(h * HEAD, HEAD)
            rows = pl.ds(half * HALF + h * HEAD, HEAD)
            qh = qn[:, h * HEAD:(h + 1) * HEAD]
            ch = ct[:, h * HEAD:(h + 1) * HEAD]
            qt[pl.ds(0, LATENT), rows] = dot(ku_ref[:, cols], transposed(qh)).astype(BF16)
            qt[pl.ds(LATENT, ROPE), rows] = rope_t[h * ROPE:(h + 1) * ROPE, :]
            dot_t[:, rows] = dot(vu_ref[:, cols], transposed(ch)).astype(BF16)

    def row_tables(half, qn, ct):
        for h in range(HEADS):
            cols = pl.ds(h * HEAD, HEAD)
            rows = pl.ds(half * HALF + h * HEAD, HEAD)
            q[rows, pl.ds(0, LATENT)] = dot(qn[:, h * HEAD:(h + 1) * HEAD], kut[cols, :]).astype(BF16)
            q[rows, pl.ds(LATENT, ROPE)] = transposed(qt[pl.ds(LATENT, ROPE), rows])
            do[rows, :] = dot(ct[:, h * HEAD:(h + 1) * HEAD], vut[cols, :]).astype(BF16)

    tables(0, qn_ref[0], qr_ref[0], ct_ref[0])

    def relay(s):
        for h in range(GPARTS):

            @pl.when(up_got(s))
            def _():
                up_copy(s, h).wait_recv()
                if s < 4:

                    @pl.when(up_sent(s + 1))
                    def _():
                        up_copy(s + 1, h).start()

            @pl.when(dn_got(s))
            def _():
                dn_copy(s, h).wait_recv()
                if s < 4:

                    @pl.when(dn_sent(s + 1))
                    def _():
                        dn_copy(s + 1, h).start()

        for slot in sorted({UP_SLOT[s], DN_SLOT[s]}):

            @pl.when(z >= NEEDS[slot])
            def _():
                sib_copy(slot).start()

    def meet(s):
        for slot in sorted({UP_SLOT[s], DN_SLOT[s]}):

            @pl.when(z >= NEEDS[slot])
            def _():
                sib_copy(slot).wait_recv()
                turn(slot)

    def turn(slot):
        for cc in range(2):
            kk[pl.ds(slot * KEYS + cc * ROWS, ROWS), :] = transposed(kt[slot, cc])

    def columns(slot, count, width):
        return jnp.concatenate(
            [kt[slot + i, cc, :width] for i in range(count) for cc in range(2)], axis=1
        )

    def forward(half, slot, count):
        rows = pl.ds(half * HALF, HALF)
        keys = pl.ds(slot * KEYS, count * KEYS)
        score = dot(kk[keys, :], qt[:, rows]) * (FACTOR * LOG2E)
        if slot == 0:
            kpos = lax.broadcasted_iota(jnp.int32, (KEYS, HALF), 0) + xh * KEYS
            lane = lax.rem(lax.broadcasted_iota(jnp.int32, (KEYS, HALF), 1), ROWS)
            qx = 1 - xh if half else xh
            score = jnp.where(kpos <= lane + (qx * KEYS + c * ROWS), score, NEG)
        dprob = dot(kk[keys, pl.ds(0, LATENT)], dot_t[:, rows])
        s_ref[keys, rows] = score
        dp_ref[keys, rows] = dprob
        top = jnp.max(score, axis=0, keepdims=True)
        if slot:
            old = st[0:1, rows]
            top = jnp.maximum(old, top)
            decay = jnp.exp2(old - top)
        e = jnp.exp2(score - top)
        total = jnp.sum(e, axis=0, keepdims=True)
        delta = jnp.sum(e * dprob, axis=0, keepdims=True)
        mixed = dot(columns(slot, count, LATENT), e.astype(BF16))
        if slot:
            total += st[1:2, rows] * decay
            delta += st[2:3, rows] * decay
            mixed += acc[:, rows] * decay
        st[0:1, rows] = top
        st[1:2, rows] = total
        st[2:3, rows] = delta
        acc[:, rows] = mixed

    def over(slot, work):
        @pl.when(z >= NEEDS[slot + 1])
        def _():
            work(slot, 2)

        @pl.when((z >= NEEDS[slot]) & (z < NEEDS[slot + 1]))
        def _():
            work(slot, 1)

    def both(slot, count):
        forward(0, slot, count)
        forward(1, slot, count)

    sib_copy(0).wait_recv()
    turn(0)
    forward(0, 0, 1)
    relay(1)
    meet(1)
    over(1, lambda slot, count: forward(0, slot, count))
    relay(2)
    for copy in query_copies:
        copy.wait_recv()
    tables(1, pqn[...], pqr[...], pct[...])
    forward(1, 0, 1)
    over(1, lambda slot, count: forward(1, slot, count))
    relay(3)
    meet(2)
    over(3, both)
    relay(4)
    meet(3)
    over(5, both)
    meet(4)

    @pl.when(z >= NEEDS[7])
    def _():
        both(7, 1)

    stats = remote(st, pst, mid_s.at[0], mid_r.at[0], partner)
    stats.start()
    for h in range(HEADS):
        cols = pl.ds(h * HEAD, HEAD)
        kut[cols, :] = transposed(ku_ref[:, cols])
        vut[cols, :] = transposed(vu_ref[:, cols])

    row_tables(0, qn_ref[0], ct_ref[0])
    row_tables(1, pqn[...], pct[...])
    dq[...] = jnp.zeros_like(dq)
    stats.wait_recv()
    for half in range(2):
        rows, other = pl.ds(half * HALF, HALF), pl.ds((1 - half) * HALF, HALF)
        top1, top2 = st[0:1, rows], pst[0:1, other]
        top = jnp.maximum(top1, top2)
        part1, part2 = jnp.exp2(top1 - top), jnp.exp2(top2 - top)
        total = st[1:2, rows] * part1 + pst[1:2, other] * part2
        fin[0:1, rows] = top + jnp.log(total) * LOG2E
        fin[1:2, rows] = (st[2:3, rows] * part1 + pst[2:3, other] * part2) / total
        fin[2:3, rows] = part1 / total

    def store_terms(column, terms):
        yy, xx = column // 2, column % 2
        terms = terms.astype(BF16)
        for zz in range(Z):
            for xxh in range(2):
                for cc in range(2):
                    first = zz * 64 + xxh * 32 + cc * 16
                    wg[cc, yy, xxh * 2 + xx, zz] = terms[first:first + 16, :]

    def backward(slot, count):
        keys = pl.ds(slot * KEYS, count * KEYS)
        cols = columns(slot, count, WIDTH)
        for half in range(2):
            rows = pl.ds(half * HALF, HALF)
            prob = jnp.exp2(s_ref[keys, rows] - fin[0:1, rows])
            w_ref[keys, rows] = prob.astype(BF16)
            dscore = (prob * (dp_ref[keys, rows] - fin[1:2, rows]) * FACTOR).astype(BF16)
            ds_ref[keys, rows] = dscore
            dq[:, rows] += dot(cols, dscore)

    def ls_copy(slot):
        return remote(dl.at[slot, 1 - c], pr.at[slot], ls_s.at[slot], ls_r.at[slot], sibling)

    def latent_terms(slot, count):
        keys = pl.ds(slot * KEYS, count * KEYS)
        a = dot(ds_ref[keys, :], q[...])
        b = dot(w_ref[keys, :], do[...])
        front = (a[:, :LATENT] + b).astype(BF16)
        for i in range(count):
            for cc in range(2):
                first = i * KEYS + cc * ROWS
                dl[slot + i, cc, pl.ds(0, ROWS), :] = front[first:first + ROWS, :]
                rope = a[first:first + ROWS, LATENT:]
                for j in range(4):
                    pair = [rope[j * 32 + n * 16:j * 32 + n * 16 + 16, :] for n in range(2)]
                    dl[slot + i, cc, pl.ds(ROWS, 16), pl.ds(j * 128, 128)] = jnp.concatenate(
                        pair, axis=1
                    ).astype(BF16)
        for i in range(count):
            ls_copy(slot + i).start()

    def strip(h):
        return pl.ds(h * RROWS, RROWS)

    def down_copy(t, h):
        return remote(
            sdn.at[t - 1, strip(h)], rdn.at[t - 1, strip(h)],
            rdn_s.at[t - 1], rdn_r.at[t - 1, h], below,
        )

    def rise_copy(t, h, src=None):
        return remote(
            sup.at[t - 1, strip(h)] if src is None else src, rup.at[t - 1, strip(h)],
            rup_s.at[t - 1], rup_r.at[t - 1, h], above,
        )

    def chip_sum(slot, h):
        return dl[slot, c, strip(h)].astype(F32) + pr[slot, strip(h)].astype(F32)

    def down_sent(t):
        return (z >= 4) & (c == 0) if t == 1 else z >= 5 - t

    def rise_sent(t):
        ok = lax.rem(z + 5 - t, Z) <= 2 + c
        return ok & (c == 1) if t == 1 else ok

    def pass_on(t):
        down_slot, rise_slot = UP_SLOT[5 - t], DN_SLOT[5 - t]
        for slot in sorted({down_slot, rise_slot}):

            @pl.when(z >= NEEDS[slot])
            def _():
                ls_copy(slot).wait_recv()

        for h in range(RPARTS):

            @pl.when(down_sent(t))
            def _():
                if t == 1:
                    sdn[t - 1, strip(h)] = chip_sum(down_slot, h).astype(BF16)
                else:
                    more = (z <= Z - 2) & (c == 0) if t == 2 else z <= Z - 2

                    @pl.when(more)
                    def _():
                        down_copy(t - 1, h).wait_recv()
                        sdn[t - 1, strip(h)] = (
                            chip_sum(down_slot, h) + rdn[t - 2, strip(h)].astype(F32)
                        ).astype(BF16)

                    @pl.when(jnp.logical_not(more))
                    def _():
                        sdn[t - 1, strip(h)] = chip_sum(down_slot, h).astype(BF16)

                down_copy(t, h).start()

            @pl.when(rise_sent(t))
            def _():
                if t == 1:
                    sup[t - 1, strip(h)] = chip_sum(rise_slot, h).astype(BF16)
                    rise_copy(t, h).start()
                else:
                    more = c == 1 if t == 2 else c >= 0
                    adds = z >= t + 3

                    @pl.when(more)
                    def _():
                        rise_copy(t - 1, h).wait_recv()

                    @pl.when(adds & more)
                    def _():
                        sup[t - 1, strip(h)] = (
                            chip_sum(rise_slot, h) + rup[t - 2, strip(h)].astype(F32)
                        ).astype(BF16)
                        rise_copy(t, h).start()

                    @pl.when(adds & jnp.logical_not(more))
                    def _():
                        sup[t - 1, strip(h)] = chip_sum(rise_slot, h).astype(BF16)
                        rise_copy(t, h).start()

                    @pl.when(jnp.logical_not(adds))
                    def _():
                        rise_copy(t, h, rup.at[t - 2, strip(h)]).start()

    def chain(slot, count):
        backward(slot, count)
        latent_terms(slot, count)

    def sides(h):
        return pl.ds(h * HEAD, HEAD), pl.ds(HALF + h * HEAD, HEAD)

    a_copies = [
        remote(wg.at[1 - c, pl.ds(2 * i, 2)], wa.at[pl.ds(2 * i, 2)], a_s.at[i], a_r.at[i], sibling)
        for i in range(2)
    ]

    def b_copy(v):
        return remote(wb.at[v], rb.at[y], b_s.at[0], b_r.at[0], at(z, x, c, v))

    three = pl.ds(0, 3)
    b_all = remote(wb.at[three], rb.at[three], b_s.at[0], b_r.at[0], above)

    def chip_weights(i):
        a_copies[i].wait_recv()
        for v in (2 * i, 2 * i + 1):
            wb[v] = (wg[c, v].astype(F32) + wa[v].astype(F32)).astype(BF16)

            @pl.when(y != v)
            def _():
                b_copy(v).start()

    c_copies = [
        remote(wc.at[v], rc.at[i], c_s.at[0], c_r.at[0], at(z, v, c, y))
        for i, v in enumerate(xpeers)
    ]
    c_all = remote(wc.at[three], rc.at[three], c_s.at[0], c_r.at[0], partner)
    d_copies = [
        remote(wd.at[v], rd.at[i], d_s.at[0], d_r.at[0], at(v, x, c, y))
        for i, v in enumerate(zpeers)
    ]

    def row_weights():
        b_all.wait_recv()
        wc[...] = (
            wb[y].astype(F32) + rb[ypeers[0]].astype(F32)
            + rb[ypeers[1]].astype(F32) + rb[ypeers[2]].astype(F32)
        ).astype(BF16)
        for copy in c_copies:
            copy.start()

    def column_weights():
        c_all.wait_recv()
        wd[...] = (
            wc[x].astype(F32) + rc[0].astype(F32) + rc[1].astype(F32) + rc[2].astype(F32)
        ).astype(BF16)
        for copy in d_copies:
            copy.start()

    def value_terms():
        for h in range(HEADS):
            cols = pl.ds(h * HEAD, HEAD)
            mine, theirs = sides(h)
            store_terms(
                4 + h, dot(ot[:, mine], ct_ref[0, :, cols]) + dot(ot[:, theirs], pct[:, cols])
            )
        a_copies[1].start()

    def key_terms():
        dqt[...] = dq[pl.ds(0, LATENT), :].astype(BF16)
        for h in range(HEADS):
            cols = pl.ds(h * HEAD, HEAD)
            mine, theirs = sides(h)
            store_terms(
                h, dot(dqt[:, mine], qn_ref[0, :, cols]) + dot(dqt[:, theirs], pqn[:, cols])
            )
        a_copies[0].start()

    att_copy = remote(asend, arecv, mid_s.at[1], mid_r.at[1], partner)
    grad_copy = remote(gsend, grecv, mid_s.at[2], mid_r.at[2], partner)

    def share_output():
        for h in range(HEADS):
            cols = pl.ds(h * HEAD, HEAD)
            mine, theirs = sides(h)
            asend[cols, :] = dot(vut[cols, :], ot[:, theirs]).astype(BF16)
            aown[cols, :] = dot(vut[cols, :], ot[:, mine])
        att_copy.start()

    def share_grads():
        for h in range(HEADS):
            cols = pl.ds(h * HEAD, HEAD)
            rope = pl.ds(LATENT + h * ROPE, ROPE)
            mine, theirs = sides(h)
            gsend[cols, :] = dot(kut[cols, :], dqt[:, theirs]).astype(BF16)
            gown[cols, :] = dot(kut[cols, :], dqt[:, mine])
            gsend[rope, :] = dq[pl.ds(LATENT, ROPE), theirs].astype(BF16)
            gown[rope, :] = dq[pl.ds(LATENT, ROPE), mine]
        grad_copy.start()

    @pl.when(z >= NEEDS[7])
    def _():
        chain(7, 1)

    over(5, backward)
    ot[...] = (acc[...] * fin[2:3, :]).astype(BF16)
    value_terms()
    over(3, backward)
    pass_on(1)
    over(1, backward)
    backward(0, 1)
    key_terms()
    chip_weights(1)
    over(5, latent_terms)
    chip_weights(0)
    share_output()
    share_grads()
    pass_on(2)
    over(3, latent_terms)
    over(1, latent_terms)
    latent_terms(0, 1)
    pass_on(3)
    row_weights()
    pass_on(4)
    column_weights()

    att_copy.wait_recv()
    grad_copy.wait_recv()
    for h in range(HEADS):
        cols = pl.ds(h * HEAD, HEAD)
        att_ref[0, :, cols] = (aown[cols, :] + arecv[cols, :].astype(F32)).T.astype(BF16)
        gn_ref[0, :, cols] = (gown[cols, :] + grecv[cols, :].astype(F32)).T.astype(BF16)
    for h in range(HEADS // 2):
        rows = pl.ds(LATENT + h * HEAD, HEAD)
        cols = pl.ds(h * HEAD, HEAD)
        gr_ref[0, :, cols] = (gown[rows, :] + grecv[rows, :].astype(F32)).T.astype(BF16)

    every = pl.ds(0, Z - 1)
    d_all = remote(wd.at[every], rd.at[every], d_s.at[0], d_r.at[0], above)
    d_all.wait_recv()
    summed = wd[z].astype(F32)
    for i in range(Z - 1):
        summed += rd[i].astype(F32)
    gw_ref[...] = summed

    ls_copy(0).wait_recv()
    for h in range(RPARTS):
        tot[strip(h), :] = chip_sum(0, h)

        @pl.when(z <= Z - 2)
        def _():
            down_copy(4, h).wait_recv()
            tot[strip(h), :] += rdn[3, strip(h)].astype(F32)

        @pl.when(z <= 2 + c)
        def _():
            rise_copy(4, h).wait_recv()
            tot[strip(h), :] += rup[3, strip(h)].astype(F32)

    folded = tot[pl.ds(ROWS, 16), :]
    rope = jnp.concatenate(
        [folded[:, j * ROPE:(j + 1) * ROPE] for j in range(LATENT // ROPE)], axis=0
    )
    gl_ref[0, pl.ds(0, LATENT), :] = tot[pl.ds(0, ROWS), :].T * scale[:LATENT, :]
    gl_ref[0, pl.ds(LATENT, ROPE), :] = rope.T * scale[LATENT:, :]

    for s in range(1, 5):

        @pl.when(up_sent(s))
        def _():
            remote(kt.at[0, 0], kt.at[0, 0], up_s.at[s - 1], up_r.at[s - 1, 0], above).wait_send()

        @pl.when(dn_sent(s))
        def _():
            remote(kt.at[0, 0], kt.at[0, 0], dn_s.at[s - 1], dn_r.at[s - 1, 0], below).wait_send()

        @pl.when(down_sent(s))
        def _():
            remote(
                sdn.at[s - 1], rdn.at[s - 1], rdn_s.at[s - 1], rdn_r.at[s - 1, 0], below
            ).wait_send()

        @pl.when(rise_sent(s))
        def _():
            remote(
                sup.at[s - 1], rup.at[s - 1], rup_s.at[s - 1], rup_r.at[s - 1, 0], above
            ).wait_send()

    for slot in range(SLOTS):

        @pl.when(z >= NEEDS[slot])
        def _():
            sib_copy(slot).wait_send()
            ls_copy(slot).wait_send()

    b_all.wait_send()

    for copy in query_copies + [stats, att_copy, grad_copy] + a_copies + [c_all, d_all]:
        copy.wait_send()


def shards(latent_values, latent_exponents, query_nope, query_rope, key_up, value_up, cotangent):
    dma = pltpu.SemaphoreType.DMA
    vmem = pl.BlockSpec(memory_space=pltpu.VMEM)
    scratch = [
        ((1, WIDTH, ROWS), BF16),
        ((1, ROWS, HALF), BF16),
        ((1, ROWS, HALF // 2), BF16),
        ((LATENT, HALF), BF16),
        ((LATENT, HALF), BF16),
        ((1, ROWS, HALF), BF16),
        ((SLOTS, 2, WIDTH, ROWS), BF16),
        ((SLOTS * KEYS, WIDTH), BF16),
        ((ROWS, HALF), BF16),
        ((ROWS, HALF // 2), BF16),
        ((ROWS, HALF), BF16),
        ((QROWS, WIDTH), BF16),
        ((WIDTH, QROWS), BF16),
        ((QROWS, LATENT), BF16),
        ((LATENT, QROWS), BF16),
        ((HALF, LATENT), BF16),
        ((HALF, LATENT), BF16),
        ((SLOTS * KEYS, QROWS), F32),
        ((SLOTS * KEYS, QROWS), F32),
        ((SLOTS * KEYS, QROWS), BF16),
        ((SLOTS * KEYS, QROWS), BF16),
        ((LATENT, QROWS), F32),
        ((WIDTH, QROWS), F32),
        ((LATENT, QROWS), BF16),
        ((LATENT, QROWS), BF16),
        ((8, QROWS), F32),
        ((8, QROWS), F32),
        ((8, QROWS), F32),
        ((HALF, ROWS), F32),
        ((HALF, ROWS), BF16),
        ((HALF, ROWS), BF16),
        ((HALF + HALF // 2, ROWS), F32),
        ((HALF + HALF // 2, ROWS), BF16),
        ((HALF + HALF // 2, ROWS), BF16),
        ((SLOTS, 2, TROWS, LATENT), BF16),
        ((SLOTS, TROWS, LATENT), BF16),
        ((4, TROWS, LATENT), BF16),
        ((4, TROWS, LATENT), BF16),
        ((4, TROWS, LATENT), BF16),
        ((4, TROWS, LATENT), BF16),
        ((TROWS, LATENT), F32),
        ((2, 4, 4, Z, 16, 128), BF16),
        ((4, 4, Z, 16, 128), BF16),
        ((4, 4, Z, 16, 128), BF16),
        ((4, 4, Z, 16, 128), BF16),
        ((4, Z, 16, 128), BF16),
        ((3, Z, 16, 128), BF16),
        ((Z, 16, 128), BF16),
        ((Z - 1, 16, 128), BF16),
    ]
    pairs = [
        ((4,), (4, GPARTS)), ((4,), (4, GPARTS)), ((SLOTS,),) * 2, ((3,),) * 2, ((3,),) * 2,
        ((SLOTS,),) * 2, ((4,), (4, RPARTS)), ((4,), (4, RPARTS)),
        ((2,),) * 2, ((1,),) * 2, ((1,),) * 2, ((1,),) * 2,
    ]
    semaphores = [dma((6,))]
    for sent, received in pairs:
        semaphores += [dma(sent), dma(received)]
    hbm = pl.BlockSpec(memory_space=pl.ANY)
    outs = pl.pallas_call(
        kernel,
        out_shape=(
            jax.ShapeDtypeStruct((1, ROWS, HALF), BF16),
            jax.ShapeDtypeStruct((1, ROWS, HALF), BF16),
            jax.ShapeDtypeStruct((1, ROWS, HALF // 2), BF16),
            jax.ShapeDtypeStruct((1, WIDTH, ROWS), F32),
            jax.ShapeDtypeStruct((16, 128), F32),
        ),
        in_specs=[hbm, pl.BlockSpec(memory_space=pltpu.SMEM)] + [hbm] * 5,
        out_specs=(vmem,) * 5,
        scratch_shapes=[pltpu.VMEM(*spec) for spec in scratch] + semaphores,
        compiler_params=pltpu.CompilerParams(
            collective_id=0, has_side_effects=True, vmem_limit_bytes=60 << 20
        ),
    )(
        jnp.swapaxes(latent_values, 1, 2), latent_exponents,
        query_nope, query_rope, key_up, value_up, cotangent,
    )
    return outs[:3] + (jnp.swapaxes(outs[3], 1, 2), outs[4])


def solution(mesh):
    block = P("dp", "ctx", None)
    return jax.shard_map(
        shards,
        mesh=mesh,
        in_specs=(block, block, block, block, P(), P(), block),
        out_specs=(block, block, block, block, P("ctx", "dp")),
        check_vma=False,
    )
```
